512 devices in a mesh: lat: 64 (over x, z_lo, core), lon: 8 (over z_hi, y).
Axes of the slice: x: 4, y: 4, z: 16 (z_hi: 2, z_lo: 8; z = z_hi * 8 + z_lo), core: 2. Of those that a mesh axis runs over, the one named last changes fastest.
Arguments:
- fine_field: bfloat16 [1, 768, 1440, 128], P(None, 'lat', 'lon'), may hold values from -6 to 6
- conv_first: bfloat16 [3, 3, 128, 128], replicated, may hold values from -0.1875 to 0.1875
- bias_first: float32 [128], replicated, may hold values from -3 to 3
- film_terms: float32 [2, 128], replicated, may hold values from -0.5 to 0.5
- conv_second: bfloat16 [3, 3, 128, 128], replicated, may hold values from -0.1875 to 0.1875
- bottleneck_in: bfloat16 [1, 3072, 1024], P(None, 'lat', 'lon'), may hold values from -6 to 6
- query_weight: bfloat16 [1024, 1024], P(None, 'lon')
- key_weight: bfloat16 [1024, 1024], P(None, 'lon')
- value_weight: bfloat16 [1024, 1024], P(None, 'lon'), may hold values from -0.1875 to 0.1875
- out_weight: bfloat16 [1024, 1024], P('lon'), may hold values from -1 to 1
Outputs:
- fine_out: bfloat16 [1, 768, 1440, 128], P(None, 'lat', 'lon')
- bottleneck_out: bfloat16 [1, 3072, 1024], P(None, 'lat', 'lon')
The draws below stay inside these ranges and needn't reach their ends.
All inputs are finite; a program needn't handle non-finite values.
Results may differ from the reference program's by a relative error of at most 0.018.
Values may be sent and summed in bfloat16 or wider, within the bound.
No kernel may reach another device: no remote copies, remote signals or barrier semaphores. Data moves between devices by JAX's collectives and lax.ppermute only.
A program may use at most 64 MiB of HBM per device.

```python
import math
import jax
import jax.numpy as jnp
from jax import lax

C = 128
D = 1024
HEADS = 16
HEAD = 64
MEMBERS = 1
NLAT = 768
NLON = 1440
TOKB = 3072


def shared_matrix(key):
    return jax.random.normal(key, (D, D), jnp.float32) / math.sqrt(D)


def draw_query_weight(key, part):
    return shared_matrix(key).astype(jnp.bfloat16)


def draw_key_weight(key, part):
    key = jax.random.fold_in(key, 7)
    own = jax.random.normal(key, (D, D), jnp.float32) / math.sqrt(D)
    return own.astype(jnp.bfloat16)


def steps_of(stream_key, shape, split, low, top_value):
    def one(axis_at, parts):
        draws = jax.random.uniform(jax.random.fold_in(jax.random.fold_in(stream_key, 6), axis_at), (parts,), jnp.float32, low / len(split), top_value / len(split))
        return jnp.repeat(jnp.exp(draws), shape[axis_at] // parts).reshape((-1,) + (1,) * (len(shape) - axis_at - 1))

    gain = one(*split[0])
    for cut in split[1:]:
        gain = gain * one(*cut)
    return gain


def noise(key, extent, spread, limit, shards=(), held_as=jnp.bfloat16):
    factor_of = steps_of(key, extent, shards, -0.22, 0.18) if shards else 1.0
    array = jax.random.normal(key, extent, jnp.float32) * spread * factor_of
    return jnp.minimum(jnp.maximum(array, -limit), limit).astype(held_as)


def setup_inputs(seed: int = 0) -> dict:
    key_list = jax.random.split(jax.random.key(seed), 11)
    return {
        "fine_field": noise(key_list[0], (MEMBERS, NLAT, NLON, C), 1.0, 6.0, ((1, 64), (2, 8))),
        "conv_first": noise(key_list[1], (3, 3, C, C), (9 * C) ** -0.5, 0.1875),
        "bias_first": noise(key_list[2], (C,), 0.5, 3.0, (), jnp.float32),
        "film_terms": jnp.clip(jax.random.uniform(key_list[3], (2, C), jnp.float32, -0.5, 0.5), -0.5, 0.5),
        "conv_second": noise(key_list[4], (3, 3, C, C), (9 * C) ** -0.5, 0.1875),
        "bottleneck_in": noise(key_list[5], (MEMBERS, TOKB, D), 1.0, 6.0, ((1, 64), (2, 8))),
        "query_weight": draw_query_weight(jax.random.fold_in(key_list[10], 71), 0),
        "key_weight": draw_key_weight(jax.random.fold_in(key_list[10], 71), 0),
        "value_weight": noise(key_list[8], (D, D), D ** -0.5, 0.1875, ((1, 8),)),
        "out_weight": noise(key_list[9], (D, D), (D // 32) ** -0.5, 1.0, ((0, 8),)),
    }


def pole_pad(field):
    half_turn = field.shape[2] // 2
    top_rows = jnp.roll(field[:, :1], half_turn, axis=2)
    bottom_rows = jnp.roll(field[:, -1:], half_turn, axis=2)
    lat_padded = jnp.concatenate([top_rows, field, bottom_rows], axis=1)
    return jnp.concatenate([lat_padded[:, :, -1:], lat_padded, lat_padded[:, :, :1]], axis=2)

def conv_valid(padded, kernel):
    return lax.conv_general_dilated(padded.astype(jnp.float32), kernel.astype(jnp.float32), (1, 1), 'VALID', dimension_numbers=('NHWC', 'HWIO', 'NHWC'), precision=lax.Precision.HIGHEST)

def reference(fine_field, conv_first, bias_first, film_terms, conv_second, bottleneck_in, query_weight, key_weight, value_weight, out_weight):

    def one_member(member_field):
        field = member_field[None]
        first = conv_valid(pole_pad(field), conv_first)
        hidden = jax.nn.silu((first + bias_first) * (1.0 + film_terms[0]) + film_terms[1]).astype(jnp.bfloat16)
        second = conv_valid(pole_pad(hidden), conv_second)
        return (field.astype(jnp.float32) + second).astype(jnp.bfloat16)[0]
    fine_out = lax.map(one_member, fine_field)
    wide = bottleneck_in.astype(jnp.float32)
    normed = (wide * lax.rsqrt(lax.optimization_barrier(jnp.mean(wide * wide, axis=-1, keepdims=True)) + 1e-06)).astype(jnp.bfloat16)
    flat_rows = normed.reshape(MEMBERS * TOKB, D)

    def project(weight):
        product = jnp.dot(flat_rows, weight, preferred_element_type=jnp.float32).astype(jnp.bfloat16)
        return product.reshape(MEMBERS, TOKB, HEADS, HEAD).transpose(2, 0, 1, 3)
    queries = project(query_weight)
    keys = project(key_weight)
    values = project(value_weight)

    def one_head(operands):
        head_q, head_k, head_v = operands
        scores = jnp.einsum('mqd,mkd->mqk', head_q.astype(jnp.float32), head_k.astype(jnp.float32)) / math.sqrt(HEAD)
        row_max = lax.optimization_barrier(jnp.max(scores, axis=-1, keepdims=True))
        expo = jnp.exp(scores - row_max)
        totals = lax.optimization_barrier(jnp.sum(expo, axis=-1, keepdims=True))
        weights = expo.astype(jnp.bfloat16)
        summed = jnp.einsum('mqk,mkd->mqd', weights.astype(jnp.float32), head_v.astype(jnp.float32))
        return (summed / totals).astype(jnp.bfloat16)
    heads_out = lax.map(one_head, (queries, keys, values))
    attended = heads_out.transpose(1, 2, 0, 3).reshape(MEMBERS * TOKB, D)
    projected = jnp.dot(attended, out_weight, preferred_element_type=jnp.float32).reshape(MEMBERS, TOKB, D)
    bottleneck_out = (wide + projected).astype(jnp.bfloat16)
    return (fine_out, bottleneck_out)
```

```python
import functools

import jax
import jax.numpy as jnp
from jax import lax
from jax.experimental import pallas as pl
from jax.experimental.pallas import tpu as pltpu
from jax.sharding import PartitionSpec as P

HEAD = 64
BF16 = jnp.bfloat16
F32 = jnp.float32
VMEM_LIMIT = 48 * 1024 * 1024


def lat_groups():
    place = lambda x, z, c: x * 16 + z * 2 + c
    over_z = [[place(x, z, c) for z in range(8)] for x in range(4) for c in range(2)]
    over_xc = [[place(x, z, c) for x in range(4) for c in range(2)] for z in range(8)]
    return over_z, over_xc


def halo_pairs(lat, lon):
    inner, outer = [], []
    for i in range(lat):
        for j in range(lon):
            me = i * lon + j
            inner.append((me, (i ^ 1) * lon + j))
            if i in (0, lat - 1):
                outer.append((me, i * lon + (j + lon // 2) % lon))
            else:
                outer.append((me, (i + 1 if i % 2 else i - 1) * lon + j))
    return inner, outer


def kernel_call(body, out_shape, **extra):
    return pl.pallas_call(
        body,
        out_shape=out_shape,
        compiler_params=pltpu.CompilerParams(vmem_limit_bytes=VMEM_LIMIT),
        **extra,
    )


def project_body(tokens_ref, wq_ref, wk_ref, wv_ref, q_ref, kv_ref):
    rows = q_ref.shape[1]
    wide = jnp.concatenate([tokens_ref[j, :rows, :] for j in range(tokens_ref.shape[0])], axis=1).astype(F32)
    normed = (wide * lax.rsqrt(jnp.mean(wide * wide, axis=-1, keepdims=True) + 1e-06)).astype(BF16)
    q = jnp.dot(normed, wq_ref[...], preferred_element_type=F32).astype(BF16)
    k = jnp.dot(normed, wk_ref[...], preferred_element_type=F32).astype(BF16)
    v = jnp.dot(normed, wv_ref[...], preferred_element_type=F32).astype(BF16)
    kv = jnp.concatenate([k, v], axis=1)
    for j in range(q_ref.shape[0]):
        q_ref[j] = q
    for j in range(kv_ref.shape[0]):
        kv_ref[j] = kv


def attend_body(q_ref, kv_ref, o_ref):
    n, rows, width = q_ref.shape
    q = q_ref[...].reshape(n * rows, width)
    kv = kv_ref[...].reshape(kv_ref.shape[0] * kv_ref.shape[1], 2 * width)
    scale = 1.0 / HEAD**0.5
    outs = []
    lane = lax.broadcasted_iota(jnp.int32, (n * rows, width), 1)
    tail = jnp.zeros((n * rows, width), F32)
    for h in range(width // HEAD):
        qh = q[:, h * HEAD : (h + 1) * HEAD]
        kh = kv[:, h * HEAD : (h + 1) * HEAD]
        vh = kv[:, width + h * HEAD : width + (h + 1) * HEAD]
        scores = lax.dot_general(qh, kh, (((1,), (1,)), ((), ())), preferred_element_type=F32) * scale
        top = jnp.max(scores, axis=-1, keepdims=True)
        expo = jnp.exp(scores - top)
        total = jnp.sum(expo, axis=-1, keepdims=True)
        outs.append(jnp.dot(expo.astype(BF16), vh, preferred_element_type=F32) / total)
        rest = top + jnp.log(total)
        for part in range(3):
            piece = rest.astype(BF16).astype(F32)
            rest = rest - piece
            tail = jnp.where(lane == 3 * h + part, piece, tail)
    o_ref[...] = jnp.concatenate(outs + [tail], axis=1).astype(BF16).reshape(o_ref.shape)


def merge_body(o_ref, wo_ref, out_ref):
    n, rows, width = o_ref.shape[0], o_ref.shape[1], o_ref.shape[2] // 2
    heads = []
    for h in range(width // HEAD):
        logs = []
        for p in range(n):
            pieces = o_ref[p, :, width : 2 * width].astype(F32)
            logs.append(pieces[:, 3 * h : 3 * h + 1] + pieces[:, 3 * h + 1 : 3 * h + 2] + pieces[:, 3 * h + 2 : 3 * h + 3])
        top = functools.reduce(jnp.maximum, logs)
        num = jnp.zeros((rows, HEAD), F32)
        total = jnp.zeros((rows, 1), F32)
        for p in range(n):
            weight = jnp.exp(logs[p] - top)
            total = total + weight
            num = num + weight * o_ref[p, :, h * HEAD : (h + 1) * HEAD].astype(F32)
        heads.append(num / total)
    attended = jnp.concatenate(heads, axis=1).astype(BF16)
    partial = jnp.dot(attended, wo_ref[...], preferred_element_type=F32).astype(BF16)
    for j in range(out_ref.shape[0]):
        out_ref[j] = partial[:, j * width : (j + 1) * width]


def finish_body(parts_ref, tokens_ref, out_ref):
    total = tokens_ref[...].astype(F32)
    shared = parts_ref[0].astype(F32)
    for j in range(1, parts_ref.shape[0]):
        shared = shared + parts_ref[j].astype(F32)
    out_ref[...] = (total + shared).astype(BF16)


def conv_valid(padded, kernel):
    return lax.conv_general_dilated(
        padded[None],
        kernel,
        (1, 1),
        "VALID",
        dimension_numbers=("NHWC", "HWIO", "NHWC"),
        preferred_element_type=F32,
    )[0]


def shards(
    fine_field,
    conv_first,
    bias_first,
    film_terms,
    conv_second,
    bottleneck_in,
    query_weight,
    key_weight,
    value_weight,
    out_weight,
):
    lats, lons = lax.axis_size("lat"), lax.axis_size("lon")
    lat, lon = lax.axis_index("lat"), lax.axis_index("lon")
    over_z, over_xc = lat_groups()
    inner, outer = halo_pairs(lats, lons)
    field, tokens = fine_field[0], bottleneck_in[0]
    height, width, channels = field.shape
    rows = tokens.shape[0]

    slot = jnp.arange(lons)[:, None, None]
    first_columns = field[:, :2].reshape(1, 2 * height, channels)
    last_columns = field[:, -2:].reshape(1, 2 * height, channels)
    columns = jnp.where(slot == (lon + 1) % lons, last_columns, first_columns)
    outgoing = jnp.concatenate([jnp.broadcast_to(tokens[None], (lons,) + tokens.shape), columns], axis=1)
    incoming = lax.all_to_all(outgoing, "lon", 0, 0)

    heads_width = query_weight.shape[1]
    n_z, n_xc = len(over_z[0]), len(over_xc[0])
    queries, pairs = kernel_call(
        project_body,
        (
            jax.ShapeDtypeStruct((n_xc, rows, heads_width), BF16),
            jax.ShapeDtypeStruct((n_z, rows, 2 * heads_width), BF16),
        ),
    )(incoming, query_weight, key_weight, value_weight)
    queries = lax.all_to_all(queries, "lat", 0, 0, axis_index_groups=over_xc)
    pairs = lax.all_to_all(pairs, "lat", 0, 0, axis_index_groups=over_z)

    before = lax.dynamic_index_in_dim(incoming, (lon + lons - 1) % lons, 0, False)[rows:].reshape(height, 2, channels)
    after = lax.dynamic_index_in_dim(incoming, (lon + 1) % lons, 0, False)[rows:].reshape(height, 2, channels)
    middle = jnp.concatenate([before, field, after], axis=1)
    even = lat % 2 == 0
    upper, lower = middle[:2], middle[-2:]
    from_inner = lax.ppermute(jnp.where(even, lower, upper), ("lat", "lon"), inner)
    from_outer = lax.ppermute(jnp.where(even, upper, lower), ("lat", "lon"), outer)
    above = jnp.where(even, from_outer, from_inner)
    below = jnp.where(even, from_inner, from_outer)
    north, south = lat == 0, lat == lats - 1
    top_window = jnp.where(
        north, jnp.concatenate([middle[:1], above]), jnp.concatenate([above, middle[:1]])
    )
    bottom_window = jnp.where(
        south, jnp.concatenate([below, middle[-1:]]), jnp.concatenate([middle[-1:], below])
    )
    row_above = jnp.where(north, above[:1], above[1:])
    row_below = jnp.where(south, below[1:], below[:1])
    stacked = jnp.concatenate([top_window, row_above, middle, row_below, bottom_window], axis=0)
    first = conv_valid(stacked, conv_first)
    hidden = jax.nn.silu((first + bias_first) * (1.0 + film_terms[0]) + film_terms[1]).astype(BF16)
    hidden = jnp.concatenate([hidden[:1], hidden[3 : 3 + height], hidden[-1:]], axis=0)
    second = conv_valid(hidden, conv_second)
    fine_out = (field.astype(F32) + second).astype(BF16)

    partial = kernel_call(
        attend_body, jax.ShapeDtypeStruct((n_xc, rows, 2 * heads_width), BF16)
    )(queries, pairs)
    partial = lax.all_to_all(partial, "lat", 0, 0, axis_index_groups=over_xc)
    projected = kernel_call(
        merge_body, jax.ShapeDtypeStruct((lons, rows, out_weight.shape[1] // lons), BF16)
    )(partial, out_weight)
    projected = lax.all_to_all(projected, "lon", 0, 0)
    bottleneck_out = kernel_call(finish_body, jax.ShapeDtypeStruct(tokens.shape, BF16))(projected, tokens)
    return (fine_out[None], bottleneck_out[None])


def solution(mesh):
    placed = (
        P(None, "lat", "lon", None),
        P(),
        P(),
        P(),
        P(),
        P(None, "lat", "lon"),
        P(None, "lon"),
        P(None, "lon"),
        P(None, "lon"),
        P("lon", None),
    )
    return jax.shard_map(
        shards,
        mesh=mesh,
        in_specs=placed,
        out_specs=(P(None, "lat", "lon", None), P(None, "lat", "lon")),
        check_vma=False,
    )
```

```python
import functools

import jax
import jax.numpy as jnp
from jax import lax
from jax.experimental import pallas as pl
from jax.experimental.pallas import tpu as pltpu
from jax.sharding import PartitionSpec as P

HEAD = 64
BF16 = jnp.bfloat16
F32 = jnp.float32
VMEM_LIMIT = 48 * 1024 * 1024


def lat_groups():
    place = lambda x, z, c: x * 16 + z * 2 + c
    over_z = [[place(x, z, c) for z in range(8)] for x in range(4) for c in range(2)]
    over_xc = [[place(x, z, c) for x in range(4) for c in range(2)] for z in range(8)]
    return over_z, over_xc


def halo_pairs(lat, lon):
    inner, outer = [], []
    for i in range(lat):
        for j in range(lon):
            me = i * lon + j
            inner.append((me, (i ^ 1) * lon + j))
            if i in (0, lat - 1):
                outer.append((me, i * lon + (j + lon // 2) % lon))
            else:
                outer.append((me, (i + 1 if i % 2 else i - 1) * lon + j))
    return inner, outer


def kernel_call(body, out_shape, **extra):
    return pl.pallas_call(
        body,
        out_shape=out_shape,
        compiler_params=pltpu.CompilerParams(vmem_limit_bytes=VMEM_LIMIT),
        **extra,
    )


def project_body(tokens_ref, weight_ref, q_ref, kv_ref):
    wide = jnp.concatenate([tokens_ref[j] for j in range(tokens_ref.shape[0])], axis=1).astype(F32)
    normed = (wide * lax.rsqrt(jnp.mean(wide * wide, axis=-1, keepdims=True) + 1e-06)).astype(BF16)
    q_width = q_ref.shape[1]
    flat = jnp.dot(normed, weight_ref[...], preferred_element_type=F32).astype(BF16)
    q_ref[...] = flat[:, :q_width]
    kv = flat[:, q_width:]
    for j in range(kv_ref.shape[0]):
        kv_ref[j] = kv


def attend_body(place_ref, q0_ref, q1_ref, q2_ref, q3_ref, kv_ref, o_ref):
    sources = (q0_ref, q1_ref, q2_ref, q3_ref)
    cores, rows, width = q0_ref.shape
    n = cores * len(sources)
    q = jnp.concatenate([ref[t] for ref in sources for t in range(cores)], axis=0)
    kv = kv_ref[...].reshape(kv_ref.shape[0] * kv_ref.shape[1], 2 * width)
    scale = 1.0 / HEAD**0.5
    outs = []
    lane = lax.broadcasted_iota(jnp.int32, (n * rows, width), 1)
    tail = jnp.zeros((n * rows, width), F32)
    for h in range(width // HEAD):
        qh = q[:, h * HEAD : (h + 1) * HEAD]
        kh = kv[:, h * HEAD : (h + 1) * HEAD]
        vh = kv[:, width + h * HEAD : width + (h + 1) * HEAD]
        scores = lax.dot_general(qh, kh, (((1,), (1,)), ((), ())), preferred_element_type=F32) * scale
        top = jnp.max(scores, axis=-1, keepdims=True)
        expo = jnp.exp(scores - top)
        total = jnp.sum(expo, axis=-1, keepdims=True)
        outs.append(jnp.dot(expo.astype(BF16), vh, preferred_element_type=F32) / total)
        rest = top + jnp.log(total)
        for part in range(3):
            piece = rest.astype(BF16).astype(F32)
            rest = rest - piece
            tail = jnp.where(lane == 3 * h + part, piece, tail)
    result = jnp.concatenate(outs + [tail], axis=1).astype(BF16)
    x, core = place_ref[0], place_ref[1]
    for s in range(len(sources)):
        for t in range(cores):
            at = lax.rem(x + s, len(sources)) * cores + (core if t == 0 else 1 - core)
            o_ref[at] = result[(s * cores + t) * rows : (s * cores + t + 1) * rows]


def merge_body(lon_ref, o_ref, wo_ref, first_ref, last_ref, out_ref):
    n, rows, width = o_ref.shape[0], o_ref.shape[1], o_ref.shape[2] // 2
    heads = []
    for h in range(width // HEAD):
        logs = []
        for p in range(n):
            pieces = o_ref[p, :, width : 2 * width].astype(F32)
            logs.append(pieces[:, 3 * h : 3 * h + 1] + pieces[:, 3 * h + 1 : 3 * h + 2] + pieces[:, 3 * h + 2 : 3 * h + 3])
        top = functools.reduce(jnp.maximum, logs)
        num = jnp.zeros((rows, HEAD), F32)
        total = jnp.zeros((rows, 1), F32)
        for p in range(n):
            weight = jnp.exp(logs[p] - top)
            total = total + weight
            num = num + weight * o_ref[p, :, h * HEAD : (h + 1) * HEAD].astype(F32)
        heads.append(num / total)
    attended = jnp.concatenate(heads, axis=1).astype(BF16)
    partial = jnp.dot(attended, wo_ref[...], preferred_element_type=F32).astype(BF16)
    lons = out_ref.shape[0]
    first, last = first_ref[...].astype(F32), last_ref[...].astype(F32)
    for j in range(lons):
        out_ref[j, :rows] = partial[:, j * width : (j + 1) * width]
        out_ref[j, rows:] = jnp.where(lax.rem(lon_ref[0] + 1, lons) == j, last, first).astype(BF16)


def three(row):
    return jnp.concatenate([pltpu.roll(row, 1, 0), row, pltpu.roll(row, row.shape[0] - 1, 0)], axis=1).astype(BF16)


def windows(wide_ref, above, rows, below, north, south):
    height = len(rows)
    wide_ref[0] = three(jnp.where(north, rows[0](), above[0]))
    wide_ref[1] = three(jnp.where(north, above[0], above[1]))
    wide_ref[2] = three(jnp.where(north, above[1], rows[0]()))
    wide_ref[3] = three(jnp.where(north, above[0], above[1]))
    for r in range(height):
        wide_ref[4 + r] = three(rows[r]())
    wide_ref[4 + height] = three(jnp.where(south, below[1], below[0]))
    wide_ref[5 + height] = three(jnp.where(south, below[0], rows[-1]()))
    wide_ref[6 + height] = three(jnp.where(south, below[1], below[0]))
    wide_ref[7 + height] = three(jnp.where(south, rows[-1](), below[1]))


def conv(source, start, count, kernel):
    _, ring, deep = source.shape
    total = None
    for dy in range(3):
        part = source[start + dy : start + dy + count].reshape(count * ring, deep)
        product = jnp.dot(part, kernel[dy], preferred_element_type=F32)
        total = product if total is None else total + product
    return total


def activate(first, bias_ref, film_ref):
    u = (first + bias_ref[...]) * (1.0 + film_ref[0:1]) + film_ref[1:2]
    return (u / (1.0 + jnp.exp(-u))).astype(BF16).astype(F32)


def conv_body(
    flags_ref, field_ref, inner_ref, outer_ref, first_ref, bias_ref, film_ref, second_ref, out_ref, wide_ref, hidden_ref
):
    height, width, channels = field_ref.shape
    ring = wide_ref.shape[1]
    north, south, even = (flags_ref[i] == 1 for i in range(3))
    gap = jnp.zeros((ring - width, channels), F32)

    def ringed(row):
        return jnp.concatenate([row.astype(F32), gap])

    def halo(i, yes_ref, no_ref):
        return ringed(jnp.where(even, yes_ref[i].astype(F32), no_ref[i].astype(F32)))

    above = [halo(i, outer_ref, inner_ref) for i in range(2)]
    below = [halo(i, inner_ref, outer_ref) for i in range(2)]
    rows = [lambda r=r: ringed(field_ref[r]) for r in range(height)]
    windows(wide_ref, above, rows, below, north, south)

    hidden_ref[0] = three(activate(conv(wide_ref, 0, 1, first_ref), bias_ref, film_ref))
    hidden_ref[height + 1] = three(activate(conv(wide_ref, height + 5, 1, first_ref), bias_ref, film_ref))
    block = 4
    for r in range(0, height, block):
        done = activate(conv(wide_ref, 3 + r, block, first_ref), bias_ref, film_ref)
        for i in range(block):
            hidden_ref[1 + r + i] = three(done[i * ring : (i + 1) * ring])
    for r in range(0, height, block):
        done = conv(hidden_ref, r, block, second_ref)
        for i in range(block):
            out_ref[r + i] = (field_ref[r + i].astype(F32) + done[i * ring : i * ring + width]).astype(BF16)


def finish_body(
    flags_ref,
    parts_ref,
    tokens_ref,
    main_ref,
    strip_ref,
    first_ref,
    bias_ref,
    film_ref,
    second_ref,
    tokens_out_ref,
    field_out_ref,
    wide_ref,
    hidden_ref,
):
    lons = parts_ref.shape[0]
    rows = tokens_ref.shape[0]
    height, width, _ = main_ref.shape
    ring = wide_ref.shape[1]
    north, south, lon = flags_ref[0] == 1, flags_ref[1] == 1, flags_ref[3]
    shared = parts_ref[0, :rows].astype(F32)
    for j in range(1, lons):
        shared = shared + parts_ref[j, :rows].astype(F32)
    tokens_out_ref[...] = (tokens_ref[...].astype(F32) + shared).astype(BF16)

    left = parts_ref[lax.rem(lon + lons - 1, lons), rows:].astype(F32)
    right = parts_ref[lax.rem(lon + 1, lons), rows:].astype(F32)
    tall = strip_ref.shape[0]

    def ringed(i):
        return jnp.concatenate(
            [strip_ref[i].astype(F32)] + [side[c * tall + i : c * tall + i + 1] for side in (right, left) for c in range(2)]
        )

    windows(
        wide_ref,
        [ringed(0), ringed(1)],
        [lambda r=r: ringed(2 + r) for r in range(height)],
        [ringed(tall - 2), ringed(tall - 1)],
        north,
        south,
    )
    done = activate(conv(wide_ref, 0, height + 6, first_ref), bias_ref, film_ref)
    for r in range(height + 2):
        at = 0 if r == 0 else height + 5 if r == height + 1 else r + 2
        hidden_ref[r] = three(done[at * ring : (at + 1) * ring])
    done = conv(hidden_ref, 0, height, second_ref)
    field_out_ref[...] = main_ref[...]
    lane = lax.broadcasted_iota(jnp.int32, (ring, done.shape[1]), 0)
    tail = width - width // ring * ring
    side = strip_ref.shape[1] // 2
    for r in range(height):
        own = jnp.concatenate([strip_ref[r + 2].astype(F32), jnp.zeros((ring - 2 * side, done.shape[1]), F32)])
        made = own + done[r * ring : (r + 1) * ring]
        field_out_ref[r, :ring] = jnp.where(lane < 2, made, main_ref[r, :ring].astype(F32)).astype(BF16)
        end = made[2 * side - tail : 2 * side]
        field_out_ref[r, width - tail :] = jnp.where(
            lane[:tail] >= tail - 2, end, main_ref[r, width - tail :].astype(F32)
        ).astype(BF16)


def shards(
    fine_field,
    conv_first,
    bias_first,
    film_terms,
    conv_second,
    bottleneck_in,
    query_weight,
    key_weight,
    value_weight,
    out_weight,
):
    lats, lons = lax.axis_size("lat"), lax.axis_size("lon")
    lat, lon = lax.axis_index("lat"), lax.axis_index("lon")
    over_z, over_xc = lat_groups()
    inner, outer = halo_pairs(lats, lons)
    field, tokens = fine_field[0], bottleneck_in[0]
    height, width, channels = field.shape
    rows = tokens.shape[0]

    incoming = lax.all_to_all(jnp.broadcast_to(tokens[None], (lons,) + tokens.shape), "lon", 0, 0)

    even = lat % 2 == 0
    weights = jnp.concatenate([query_weight, key_weight, value_weight], axis=1)
    upper, lower, weights = lax.optimization_barrier((field[:2], field[-2:], weights))
    from_inner = lax.ppermute(jnp.where(even, lower, upper), ("lat", "lon"), inner)
    from_outer = lax.ppermute(jnp.where(even, upper, lower), ("lat", "lon"), outer)
    above = jnp.where(even, from_outer, from_inner)
    below = jnp.where(even, from_inner, from_outer)

    heads_width = query_weight.shape[1]
    n_z, n_xc = len(over_z[0]), len(over_xc[0])
    queries, pairs = kernel_call(
        project_body,
        (
            jax.ShapeDtypeStruct((rows, heads_width), BF16),
            jax.ShapeDtypeStruct((n_z, rows, 2 * heads_width), BF16),
        ),
    )(incoming, weights)
    pairs = lax.all_to_all(pairs, "lat", 0, 0, axis_index_groups=over_z)
    other = lax.ppermute(queries, "lat", [(i, i ^ 1) for i in range(lats)])
    chip = jnp.stack([queries, other])
    step = lats // 4
    gathered = [chip] + [
        lax.ppermute(chip, "lat", [(i, (i - s * step) % lats) for i in range(lats)]) for s in range(1, 4)
    ]

    place = jnp.stack([lat // step, lat % 2]).astype(jnp.int32)
    partial = pl.pallas_call(
        attend_body,
        in_specs=[pl.BlockSpec(memory_space=pltpu.SMEM)] + [pl.BlockSpec(memory_space=pltpu.VMEM)] * 5,
        out_shape=jax.ShapeDtypeStruct((n_xc, rows, 2 * heads_width), BF16),
        compiler_params=pltpu.CompilerParams(vmem_limit_bytes=VMEM_LIMIT),
    )(place, *gathered, pairs)

    partial = lax.all_to_all(partial, "lat", 0, 0, axis_index_groups=over_xc)
    side = 6
    ends = lambda rows: jnp.concatenate([rows[:, :side], rows[:, -side:]], axis=1)
    strip = jnp.concatenate([ends(above), ends(field), ends(below)])
    tall = height + 4
    first_columns = jnp.concatenate([strip[:, 0], strip[:, 1]])
    last_columns = jnp.concatenate([strip[:, -2], strip[:, -1]])
    smem, vmem = pl.BlockSpec(memory_space=pltpu.SMEM), pl.BlockSpec(memory_space=pltpu.VMEM)
    params = pltpu.CompilerParams(vmem_limit_bytes=VMEM_LIMIT)
    projected = pl.pallas_call(
        merge_body,
        in_specs=[smem] + [vmem] * 4,
        out_shape=jax.ShapeDtypeStruct((lons, rows + 2 * tall, out_weight.shape[1] // lons), BF16),
        compiler_params=params,
    )(lon.reshape(1).astype(jnp.int32), partial, out_weight, first_columns, last_columns)
    projected = lax.all_to_all(projected, "lon", 0, 0)

    flags = jnp.stack([lat == 0, lat == lats - 1, even, lon]).astype(jnp.int32)
    kernels = (
        conv_first.reshape(3, 3 * channels, channels),
        bias_first.reshape(1, channels),
        film_terms,
        conv_second.reshape(3, 3 * channels, channels),
    )
    ring = -(-width // 16) * 16
    main = pl.pallas_call(
        conv_body,
        in_specs=[smem] + [vmem] * 7,
        out_shape=jax.ShapeDtypeStruct(field.shape, BF16),
        scratch_shapes=[
            pltpu.VMEM((height + 8, ring, 3 * channels), BF16),
            pltpu.VMEM((height + 2, ring, 3 * channels), BF16),
        ],
        compiler_params=params,
    )(flags, field, from_inner, from_outer, *kernels)
    bottleneck_out, fine_out = pl.pallas_call(
        finish_body,
        in_specs=[smem] + [vmem] * 8,
        out_shape=(jax.ShapeDtypeStruct(tokens.shape, BF16), jax.ShapeDtypeStruct(field.shape, BF16)),
        scratch_shapes=[
            pltpu.VMEM((height + 8, 2 * side + 4, 3 * channels), BF16),
            pltpu.VMEM((height + 2, 2 * side + 4, 3 * channels), BF16),
        ],
        compiler_params=params,
    )(flags, projected, tokens, main, strip, *kernels)
    return (fine_out[None], bottleneck_out[None])


def solution(mesh):
    placed = (
        P(None, "lat", "lon", None),
        P(),
        P(),
        P(),
        P(),
        P(None, "lat", "lon"),
        P(None, "lon"),
        P(None, "lon"),
        P(None, "lon"),
        P("lon", None),
    )
    return jax.shard_map(
        shards,
        mesh=mesh,
        in_specs=placed,
        out_specs=(P(None, "lat", "lon", None), P(None, "lat", "lon")),
        check_vma=False,
    )
```

```python
import functools

import jax
import jax.numpy as jnp
from jax import lax
from jax.experimental import pallas as pl
from jax.experimental.pallas import tpu as pltpu
from jax.sharding import PartitionSpec as P

HEAD = 64
BF16 = jnp.bfloat16
F32 = jnp.float32
VMEM_LIMIT = 48 * 1024 * 1024


def lat_groups():
    place = lambda x, z, c: x * 16 + z * 2 + c
    over_z = [[place(x, z, c) for z in (4, 3, 5, 2, 6, 1, 7, 0)] for x in range(4) for c in range(2)]
    over_xc = [[place(x, z, c) for x in range(4) for c in range(2)] for z in range(8)]
    return over_z, over_xc


def halo_pairs(lat, lon):
    inner, outer = [], []
    for i in range(lat):
        for j in range(lon):
            me = i * lon + j
            inner.append((me, (i ^ 1) * lon + j))
            if i in (0, lat - 1):
                outer.append((me, i * lon + (j + lon // 2) % lon))
            else:
                outer.append((me, (i + 1 if i % 2 else i - 1) * lon + j))
    return inner, outer


def kernel_call(body, out_shape, **extra):
    return pl.pallas_call(
        body,
        out_shape=out_shape,
        compiler_params=pltpu.CompilerParams(vmem_limit_bytes=VMEM_LIMIT),
        **extra,
    )


def spread_body(flags_ref, given_ref, out_ref):
    lons, total = out_ref.shape[:2]
    half = given_ref.shape[0] - total
    rows = total - half
    first, last = given_ref[rows:total].astype(F32), given_ref[total:].astype(F32)
    for j in range(lons):
        out_ref[j, :rows] = given_ref[:rows]
        out_ref[j, rows:] = jnp.where(lax.rem(flags_ref[3] + 1 + lons // 2, lons) == j, last, first).astype(BF16)


def project_body(tokens_ref, weight_ref, q_ref, kv_ref):
    rows = q_ref.shape[0]
    wide = jnp.concatenate([tokens_ref[(j + tokens_ref.shape[0] // 2) % tokens_ref.shape[0], :rows] for j in range(tokens_ref.shape[0])], axis=1).astype(F32)
    normed = (wide * lax.rsqrt(jnp.mean(wide * wide, axis=-1, keepdims=True) + 1e-06)).astype(BF16)
    q_width = q_ref.shape[1]
    flat = jnp.dot(normed, weight_ref[...], preferred_element_type=F32).astype(BF16)
    q_ref[...] = flat[:, :q_width]
    kv = flat[:, q_width:]
    for j in range(kv_ref.shape[0]):
        kv_ref[j] = kv


def attend_body(flags_ref, own_ref, other_ref, kv_ref, o_ref):
    rows, width = own_ref.shape[1:]
    q = jnp.concatenate([own_ref[...], other_ref[...]], axis=0)
    n = q.shape[0]
    q = q.reshape(n * rows, width)
    kv = kv_ref[...].reshape(kv_ref.shape[0] * kv_ref.shape[1], 2 * width)
    scale = 1.0 / HEAD**0.5
    outs = []
    lane = lax.broadcasted_iota(jnp.int32, (n * rows, width), 1)
    tail = jnp.zeros((n * rows, width), F32)
    for h in range(width // HEAD):
        qh = q[:, h * HEAD : (h + 1) * HEAD]
        kh = kv[:, h * HEAD : (h + 1) * HEAD]
        vh = kv[:, width + h * HEAD : width + (h + 1) * HEAD]
        scores = lax.dot_general(qh, kh, (((1,), (1,)), ((), ())), preferred_element_type=F32) * scale
        top = jnp.max(scores, axis=-1, keepdims=True)
        expo = jnp.exp(scores - top)
        total = jnp.sum(expo, axis=-1, keepdims=True)
        outs.append(jnp.dot(expo.astype(BF16), vh, preferred_element_type=F32) / total)
        rest = top + jnp.log(total)
        for part in range(3):
            piece = rest.astype(BF16).astype(F32)
            rest = rest - piece
            tail = jnp.where(lane == 3 * h + part, piece, tail)
    result = jnp.concatenate(outs + [tail], axis=1).astype(BF16)
    x, core = flags_ref[4], flags_ref[5]
    for t in range(2):
        for s, chip in enumerate((x, x ^ 1, 3 - x, (3 - x) ^ 1)):
            o_ref[2 * chip + (core ^ t)] = result[(4 * t + s) * rows : (4 * t + s + 1) * rows]


def merge_body(flags_ref, o_ref, wo_hbm, first_ref, last_ref, out_ref, wo_ref, wo_sem):
    copy = pltpu.make_async_copy(wo_hbm, wo_ref, wo_sem)
    copy.start()
    n, rows, width = o_ref.shape[0], o_ref.shape[1], o_ref.shape[2] // 2
    heads = []
    for h in range(width // HEAD):
        logs = []
        for p in range(n):
            pieces = o_ref[p, :, width : 2 * width].astype(F32)
            logs.append(pieces[:, 3 * h : 3 * h + 1] + pieces[:, 3 * h + 1 : 3 * h + 2] + pieces[:, 3 * h + 2 : 3 * h + 3])
        top = functools.reduce(jnp.maximum, logs)
        num = jnp.zeros((rows, HEAD), F32)
        total = jnp.zeros((rows, 1), F32)
        for p in range(n):
            weight = jnp.exp(logs[p] - top)
            total = total + weight
            num = num + weight * o_ref[p, :, h * HEAD : (h + 1) * HEAD].astype(F32)
        heads.append(num / total)
    attended = jnp.concatenate(heads, axis=1).astype(BF16)
    copy.wait()
    partial = jnp.dot(attended, wo_ref[...], preferred_element_type=F32).astype(BF16)
    lons = out_ref.shape[0]
    first, last = first_ref[...].astype(F32), last_ref[...].astype(F32)
    for j in range(lons):
        at = (j + lons // 2) % lons
        out_ref[at, :rows] = partial[:, j * width : (j + 1) * width]
        out_ref[at, rows:] = jnp.where(lax.rem(flags_ref[3] + 1, lons) == j, last, first).astype(BF16)


def three(row):
    return jnp.concatenate([pltpu.roll(row, 1, 0), row, pltpu.roll(row, row.shape[0] - 1, 0)], axis=1).astype(BF16)


def windows(wide_ref, above, rows, below, north, south):
    height = len(rows)
    wide_ref[0] = three(jnp.where(north, rows[0](), above[0]))
    wide_ref[1] = three(jnp.where(north, above[0], above[1]))
    wide_ref[2] = three(jnp.where(north, above[1], rows[0]()))
    wide_ref[3] = three(jnp.where(north, above[0], above[1]))
    for r in range(height):
        wide_ref[4 + r] = three(rows[r]())
    wide_ref[4 + height] = three(jnp.where(south, below[1], below[0]))
    wide_ref[5 + height] = three(jnp.where(south, below[0], rows[-1]()))
    wide_ref[6 + height] = three(jnp.where(south, below[1], below[0]))
    wide_ref[7 + height] = three(jnp.where(south, rows[-1](), below[1]))


def conv(source, start, count, kernel):
    _, ring, deep = source.shape
    total = None
    for dy in range(3):
        part = source[start + dy : start + dy + count].reshape(count * ring, deep)
        product = jnp.dot(part, kernel[dy], preferred_element_type=F32)
        total = product if total is None else total + product
    return total


def activate(first, bias_ref, film_ref):
    u = (first + bias_ref[...]) * (1.0 + film_ref[0:1]) + film_ref[1:2]
    return (u / (1.0 + jnp.exp(-u))).astype(BF16).astype(F32)


def conv_body(
    flags_ref, field_ref, inner_ref, outer_ref, first_ref, bias_ref, film_ref, second_ref, out_ref, wide_ref, hidden_ref
):
    height, width, channels = field_ref.shape
    ring = wide_ref.shape[1]
    north, south, even = (flags_ref[i] == 1 for i in range(3))
    gap = jnp.zeros((ring - width, channels), F32)

    def ringed(row):
        return jnp.concatenate([row.astype(F32), gap])

    def halo(i, yes_ref, no_ref):
        return ringed(jnp.where(even, yes_ref[i].astype(F32), no_ref[i].astype(F32)))

    above = [halo(i, outer_ref, inner_ref) for i in range(2)]
    below = [halo(i, inner_ref, outer_ref) for i in range(2)]
    rows = [lambda r=r: ringed(field_ref[r]) for r in range(height)]
    windows(wide_ref, above, rows, below, north, south)

    hidden_ref[0] = three(activate(conv(wide_ref, 0, 1, first_ref), bias_ref, film_ref))
    hidden_ref[height + 1] = three(activate(conv(wide_ref, height + 5, 1, first_ref), bias_ref, film_ref))
    block = 4
    for r in range(0, height, block):
        done = activate(conv(wide_ref, 3 + r, block, first_ref), bias_ref, film_ref)
        for i in range(block):
            hidden_ref[1 + r + i] = three(done[i * ring : (i + 1) * ring])
    for r in range(0, height, block):
        done = conv(hidden_ref, r, block, second_ref)
        for i in range(block):
            out_ref[r + i] = (field_ref[r + i].astype(F32) + done[i * ring : i * ring + width]).astype(BF16)


def finish_body(
    flags_ref,
    parts_ref,
    incoming_ref,
    tokens_ref,
    main_ref,
    strip_ref,
    first_ref,
    bias_ref,
    film_ref,
    second_ref,
    tokens_out_ref,
    field_out_ref,
    wide_ref,
    hidden_ref,
):
    lons = parts_ref.shape[0]
    rows = tokens_ref.shape[0]
    height, width, _ = main_ref.shape
    ring = wide_ref.shape[1]
    north, south, lon = flags_ref[0] == 1, flags_ref[1] == 1, flags_ref[3]
    shared = parts_ref[0, :rows].astype(F32)
    for j in range(1, lons):
        shared = shared + parts_ref[j, :rows].astype(F32)
    tokens_out_ref[...] = (tokens_ref[...].astype(F32) + shared).astype(BF16)

    before, after = lax.rem(lon + lons - 1, lons), lax.rem(lon + 1, lons)
    corners = [parts_ref[lax.rem(at + lons // 2, lons), rows:].astype(F32) for at in (after, before)]
    sides = [incoming_ref[lax.rem(at + lons // 2, lons), rows:].astype(F32) for at in (after, before)]
    tall = strip_ref.shape[0]

    def ringed(i):
        inside = 2 <= i < tall - 2
        held, at, step = (sides, i - 2, height) if inside else (corners, i if i < 2 else i - height, 4)
        return jnp.concatenate(
            [strip_ref[i].astype(F32)] + [side[c * step + at : c * step + at + 1] for side in held for c in range(2)]
        )

    windows(
        wide_ref,
        [ringed(0), ringed(1)],
        [lambda r=r: ringed(2 + r) for r in range(height)],
        [ringed(tall - 2), ringed(tall - 1)],
        north,
        south,
    )
    done = activate(conv(wide_ref, 0, height + 6, first_ref), bias_ref, film_ref)
    for r in range(height + 2):
        at = 0 if r == 0 else height + 5 if r == height + 1 else r + 2
        hidden_ref[r] = three(done[at * ring : (at + 1) * ring])
    done = conv(hidden_ref, 0, height, second_ref)
    field_out_ref[...] = main_ref[...]
    lane = lax.broadcasted_iota(jnp.int32, (ring, done.shape[1]), 0)
    tail = width - width // ring * ring
    side = strip_ref.shape[1] // 2
    for r in range(height):
        own = jnp.concatenate([strip_ref[r + 2].astype(F32), jnp.zeros((ring - 2 * side, done.shape[1]), F32)])
        made = own + done[r * ring : (r + 1) * ring]
        field_out_ref[r, :ring] = jnp.where(lane < 2, made, main_ref[r, :ring].astype(F32)).astype(BF16)
        end = made[2 * side - tail : 2 * side]
        field_out_ref[r, width - tail :] = jnp.where(
            lane[:tail] >= tail - 2, end, main_ref[r, width - tail :].astype(F32)
        ).astype(BF16)


def shards(
    fine_field,
    conv_first,
    bias_first,
    film_terms,
    conv_second,
    bottleneck_in,
    query_weight,
    key_weight,
    value_weight,
    out_weight,
):
    lats, lons = lax.axis_size("lat"), lax.axis_size("lon")
    lat, lon = lax.axis_index("lat"), lax.axis_index("lon")
    over_z, over_xc = lat_groups()
    inner, outer = halo_pairs(lats, lons)
    field, tokens = fine_field[0], bottleneck_in[0]
    height, width, channels = field.shape
    rows = tokens.shape[0]

    even = lat % 2 == 0
    step = lats // 4
    flags = jnp.stack([lat == 0, lat == lats - 1, even, lon, lat // step, lat % 2]).astype(jnp.int32)

    turned = [[(j + lons // 2) % lons for j in range(lons)]]
    smem, vmem = pl.BlockSpec(memory_space=pltpu.SMEM), pl.BlockSpec(memory_space=pltpu.VMEM)
    params = pltpu.CompilerParams(vmem_limit_bytes=VMEM_LIMIT)
    column = lambda c: field[:, c]
    spread = pl.pallas_call(
        spread_body,
        in_specs=[smem, vmem],
        out_shape=jax.ShapeDtypeStruct((lons, rows + 2 * height, channels), BF16),
        compiler_params=params,
    )(
        flags,
        jnp.concatenate([tokens] + [column(c) for c in (0, 1, width - 2, width - 1)]),
    )
    incoming = lax.all_to_all(spread, "lon", 0, 0, axis_index_groups=turned)

    weights = jnp.concatenate([query_weight, key_weight, value_weight], axis=1)
    upper, lower, weights, flags = lax.optimization_barrier((field[:2], field[-2:], weights, flags))
    from_inner = lax.ppermute(jnp.where(even, lower, upper), ("lat", "lon"), inner)
    from_outer = lax.ppermute(jnp.where(even, upper, lower), ("lat", "lon"), outer)

    heads_width = query_weight.shape[1]
    n_z, n_xc = len(over_z[0]), len(over_xc[0])
    queries, pairs = kernel_call(
        project_body,
        (
            jax.ShapeDtypeStruct((rows, heads_width), BF16),
            jax.ShapeDtypeStruct((n_z, rows, 2 * heads_width), BF16),
        ),
    )(incoming, weights)
    pairs = lax.all_to_all(pairs, "lat", 0, 0, axis_index_groups=over_z)
    swap = lambda v, to: lax.ppermute(v, "lat", [(i, to(i // step) * step + i % step) for i in range(lats)])
    near = swap(queries, lambda x: x ^ 1)
    from_inner, from_outer, near = lax.optimization_barrier((from_inner, from_outer, near))
    above = jnp.where(even, from_outer, from_inner)
    below = jnp.where(even, from_inner, from_outer)
    two = jnp.stack([queries, near])
    own = jnp.concatenate([two, swap(two, lambda x: 3 - x)])
    other = lax.ppermute(own, "lat", [(i, i ^ 1) for i in range(lats)])

    side = 6
    ends = lambda rows: jnp.concatenate([rows[:, :side], rows[:, -side:]], axis=1)
    corners = jnp.concatenate([ends(above), ends(below)])
    strip = jnp.concatenate([corners[:2], ends(field), corners[2:]])
    first_columns = jnp.concatenate([corners[:, 0], corners[:, 1]])
    last_columns = jnp.concatenate([corners[:, -2], corners[:, -1]])
    first_columns, last_columns, own = lax.optimization_barrier((first_columns, last_columns, own))

    partial = pl.pallas_call(
        attend_body,
        in_specs=[pl.BlockSpec(memory_space=pltpu.SMEM)] + [pl.BlockSpec(memory_space=pltpu.VMEM)] * 3,
        out_shape=jax.ShapeDtypeStruct((n_xc, rows, 2 * heads_width), BF16),
        compiler_params=pltpu.CompilerParams(vmem_limit_bytes=VMEM_LIMIT),
    )(flags, own, other, pairs)

    partial = lax.all_to_all(partial, "lat", 0, 0, axis_index_groups=over_xc)
    projected = pl.pallas_call(
        merge_body,
        in_specs=[smem, vmem, pl.BlockSpec(memory_space=pl.ANY), vmem, vmem],
        out_shape=jax.ShapeDtypeStruct((lons, rows + first_columns.shape[0], out_weight.shape[1] // lons), BF16),
        scratch_shapes=[pltpu.VMEM(out_weight.shape, BF16), pltpu.SemaphoreType.DMA],
        compiler_params=params,
    )(flags, partial, out_weight, first_columns, last_columns)
    projected = lax.all_to_all(projected, "lon", 0, 0, axis_index_groups=turned)

    kernels = (
        conv_first.reshape(3, 3 * channels, channels),
        bias_first.reshape(1, channels),
        film_terms,
        conv_second.reshape(3, 3 * channels, channels),
    )
    ring = -(-width // 16) * 16
    main = pl.pallas_call(
        conv_body,
        in_specs=[smem] + [vmem] * 7,
        out_shape=jax.ShapeDtypeStruct(field.shape, BF16),
        scratch_shapes=[
            pltpu.VMEM((height + 8, ring, 3 * channels), BF16),
            pltpu.VMEM((height + 2, ring, 3 * channels), BF16),
        ],
        compiler_params=params,
    )(flags, field, from_inner, from_outer, *kernels)
    bottleneck_out, fine_out = pl.pallas_call(
        finish_body,
        in_specs=[smem] + [vmem] * 9,
        out_shape=(jax.ShapeDtypeStruct(tokens.shape, BF16), jax.ShapeDtypeStruct(field.shape, BF16)),
        scratch_shapes=[
            pltpu.VMEM((height + 8, 2 * side + 4, 3 * channels), BF16),
            pltpu.VMEM((height + 2, 2 * side + 4, 3 * channels), BF16),
        ],
        compiler_params=params,
    )(flags, projected, incoming, tokens, main, strip, *kernels)
    return (fine_out[None], bottleneck_out[None])


def solution(mesh):
    placed = (
        P(None, "lat", "lon", None),
        P(),
        P(),
        P(),
        P(),
        P(None, "lat", "lon"),
        P(None, "lon"),
        P(None, "lon"),
        P(None, "lon"),
        P("lon", None),
    )
    return jax.shard_map(
        shards,
        mesh=mesh,
        in_specs=placed,
        out_specs=(P(None, "lat", "lon", None), P(None, "lat", "lon")),
        check_vma=False,
    )
```

```python
import functools

import jax
import jax.numpy as jnp
from jax import lax
from jax.experimental import pallas as pl
from jax.experimental.pallas import tpu as pltpu
from jax.sharding import PartitionSpec as P

HEAD = 64
BF16 = jnp.bfloat16
F32 = jnp.float32
VMEM_LIMIT = 48 * 1024 * 1024


def lat_groups():
    place = lambda x, z, c: x * 16 + z * 2 + c
    over_z = [[place(x, z, c) for z in (4, 3, 5, 2, 6, 1, 7, 0)] for x in range(4) for c in range(2)]
    over_xc = [[place(x, z, c) for x in range(4) for c in range(2)] for z in range(8)]
    return over_z, over_xc


def halo_pairs(lat, lon):
    inner, outer = [], []
    for i in range(lat):
        for j in range(lon):
            me = i * lon + j
            inner.append((me, (i ^ 1) * lon + j))
            if i in (0, lat - 1):
                outer.append((me, i * lon + (j + lon // 2) % lon))
            else:
                outer.append((me, (i + 1 if i % 2 else i - 1) * lon + j))
    return inner, outer


def place_here():
    return lax.axis_index("lat"), lax.axis_index("lon")


def spot(lon):
    return 7 - lon


def kernel_call(body, out_shape, **extra):
    return pl.pallas_call(
        body,
        out_shape=out_shape,
        compiler_params=pltpu.CompilerParams(vmem_limit_bytes=VMEM_LIMIT),
        **extra,
    )


def spread_body(tokens_hbm, given_ref, out_ref, tokens_ref, sem):
    copy = pltpu.make_async_copy(tokens_hbm, tokens_ref, sem)
    copy.start()
    lon = place_here()[1]
    lons, total = out_ref.shape[:2]
    rows = tokens_ref.shape[0]
    first, last = given_ref[: total - rows].astype(F32), given_ref[total - rows :].astype(F32)
    for j in range(lons):
        out_ref[j, rows:] = jnp.where(spot(lax.rem(lon + 1, lons)) == j, last, first).astype(BF16)
    copy.wait()
    for j in range(lons):
        out_ref[j, :rows] = tokens_ref[...]


def project_body(tokens_ref, weight_ref, q_ref, kv_ref):
    rows = q_ref.shape[0]
    wide = jnp.concatenate([tokens_ref[spot(j), :rows] for j in range(tokens_ref.shape[0])], axis=1).astype(F32)
    normed = (wide * lax.rsqrt(jnp.mean(wide * wide, axis=-1, keepdims=True) + 1e-06)).astype(BF16)
    q_width = q_ref.shape[1]
    flat = jnp.dot(normed, weight_ref[...], preferred_element_type=F32).astype(BF16)
    q_ref[...] = flat[:, :q_width]
    kv = flat[:, q_width:]
    for j in range(kv_ref.shape[0]):
        kv_ref[j] = kv


def attend_body(own_ref, other_ref, kv_ref, o_ref):
    rows, width = own_ref.shape[1:]
    q = jnp.concatenate([own_ref[...], other_ref[...]], axis=0)
    n = q.shape[0]
    q = q.reshape(n * rows, width)
    kv = kv_ref[...].reshape(kv_ref.shape[0] * kv_ref.shape[1], 2 * width)
    scale = 1.0 / HEAD**0.5
    outs = []
    lane = lax.broadcasted_iota(jnp.int32, (n * rows, width), 1)
    tail = jnp.zeros((n * rows, width), F32)
    for h in range(width // HEAD):
        qh = q[:, h * HEAD : (h + 1) * HEAD]
        kh = kv[:, h * HEAD : (h + 1) * HEAD]
        vh = kv[:, width + h * HEAD : width + (h + 1) * HEAD]
        scores = lax.dot_general(qh, kh, (((1,), (1,)), ((), ())), preferred_element_type=F32) * scale
        top = jnp.max(scores, axis=-1, keepdims=True)
        expo = jnp.exp(scores - top)
        total = jnp.sum(expo, axis=-1, keepdims=True)
        outs.append(jnp.dot(expo.astype(BF16), vh, preferred_element_type=F32) / total)
        rest = top + jnp.log(total)
        for part in range(3):
            piece = rest.astype(BF16).astype(F32)
            rest = rest - piece
            tail = jnp.where(lane == 3 * h + part, piece, tail)
    result = jnp.concatenate(outs + [tail], axis=1).astype(BF16)
    lat = place_here()[0]
    x, core = lat // 16, lax.rem(lat, 2)
    for t in range(2):
        for s, chip in enumerate((x, x ^ 1, 3 - x, (3 - x) ^ 1)):
            o_ref[2 * chip + (core ^ t)] = result[(4 * t + s) * rows : (4 * t + s + 1) * rows]


def merge_body(o_ref, wo_ref, first_ref, last_ref, out_ref):
    lon = place_here()[1]
    n, rows, width = o_ref.shape[0], o_ref.shape[1], o_ref.shape[2] // 2
    heads = []
    for h in range(width // HEAD):
        logs = []
        for p in range(n):
            pieces = o_ref[p, :, width : 2 * width].astype(F32)
            logs.append(pieces[:, 3 * h : 3 * h + 1] + pieces[:, 3 * h + 1 : 3 * h + 2] + pieces[:, 3 * h + 2 : 3 * h + 3])
        top = functools.reduce(jnp.maximum, logs)
        num = jnp.zeros((rows, HEAD), F32)
        total = jnp.zeros((rows, 1), F32)
        for p in range(n):
            weight = jnp.exp(logs[p] - top)
            total = total + weight
            num = num + weight * o_ref[p, :, h * HEAD : (h + 1) * HEAD].astype(F32)
        heads.append(num / total)
    attended = jnp.concatenate(heads, axis=1).astype(BF16)
    partial = jnp.dot(attended, wo_ref[...], preferred_element_type=F32).astype(BF16)
    lons = out_ref.shape[0]
    first, last = first_ref[...].astype(F32), last_ref[...].astype(F32)
    for j in range(lons):
        at = spot(j)
        out_ref[at, :rows] = partial[:, j * width : (j + 1) * width]
        out_ref[at, rows:] = jnp.where(lax.rem(lon + 1, lons) == j, last, first).astype(BF16)


def three(row):
    return jnp.concatenate([pltpu.roll(row, 1, 0), row, pltpu.roll(row, row.shape[0] - 1, 0)], axis=1).astype(BF16)


def windows(wide_ref, above, rows, below, north, south):
    height = len(rows)
    wide_ref[0] = three(jnp.where(north, rows[0](), above[0]))
    wide_ref[1] = three(jnp.where(north, above[0], above[1]))
    wide_ref[2] = three(jnp.where(north, above[1], rows[0]()))
    wide_ref[3] = three(jnp.where(north, above[0], above[1]))
    for r in range(height):
        wide_ref[4 + r] = three(rows[r]())
    wide_ref[4 + height] = three(jnp.where(south, below[1], below[0]))
    wide_ref[5 + height] = three(jnp.where(south, below[0], rows[-1]()))
    wide_ref[6 + height] = three(jnp.where(south, below[1], below[0]))
    wide_ref[7 + height] = three(jnp.where(south, rows[-1](), below[1]))


def conv(source, start, count, kernel):
    _, ring, deep = source.shape
    total = None
    for dy in range(3):
        part = source[start + dy : start + dy + count].reshape(count * ring, deep)
        product = jnp.dot(part, kernel[dy], preferred_element_type=F32)
        total = product if total is None else total + product
    return total


def activate(first, bias_ref, film_ref):
    u = (first + bias_ref[...]) * (1.0 + film_ref[0:1]) + film_ref[1:2]
    return (u / (1.0 + jnp.exp(-u))).astype(BF16).astype(F32)


def conv_body(
    field_ref, inner_ref, outer_ref, first_ref, bias_ref, film_ref, second_ref, out_ref, wide_ref, hidden_ref
):
    height, width, channels = field_ref.shape
    ring = wide_ref.shape[1]
    lat = place_here()[0]
    north, south, even = lat == 0, lat == lax.axis_size("lat") - 1, lax.rem(lat, 2) == 0
    gap = jnp.zeros((ring - width, channels), F32)

    def ringed(row):
        return jnp.concatenate([row.astype(F32), gap])

    def halo(i, yes_ref, no_ref):
        return ringed(jnp.where(even, yes_ref[i].astype(F32), no_ref[i].astype(F32)))

    above = [halo(i, outer_ref, inner_ref) for i in range(2)]
    below = [halo(i, inner_ref, outer_ref) for i in range(2)]
    rows = [lambda r=r: ringed(field_ref[r]) for r in range(height)]
    windows(wide_ref, above, rows, below, north, south)

    hidden_ref[0] = three(activate(conv(wide_ref, 0, 1, first_ref), bias_ref, film_ref))
    hidden_ref[height + 1] = three(activate(conv(wide_ref, height + 5, 1, first_ref), bias_ref, film_ref))
    block = 4
    for r in range(0, height, block):
        done = activate(conv(wide_ref, 3 + r, block, first_ref), bias_ref, film_ref)
        for i in range(block):
            hidden_ref[1 + r + i] = three(done[i * ring : (i + 1) * ring])
    for r in range(0, height, block):
        done = conv(hidden_ref, r, block, second_ref)
        for i in range(block):
            out_ref[r + i] = (field_ref[r + i].astype(F32) + done[i * ring : i * ring + width]).astype(BF16)


def finish_body(
    parts_ref,
    incoming_ref,
    tokens_ref,
    main_ref,
    strip_ref,
    first_ref,
    bias_ref,
    film_ref,
    second_ref,
    tokens_out_ref,
    field_out_ref,
    wide_ref,
    hidden_ref,
):
    lons = parts_ref.shape[0]
    rows = tokens_ref.shape[0]
    height, width, _ = main_ref.shape
    ring = wide_ref.shape[1]
    lat, lon = place_here()
    north, south = lat == 0, lat == lax.axis_size("lat") - 1
    shared = parts_ref[0, :rows].astype(F32)
    for j in range(1, lons):
        shared = shared + parts_ref[j, :rows].astype(F32)
    tokens_out_ref[...] = (tokens_ref[...].astype(F32) + shared).astype(BF16)

    before, after = lax.rem(lon + lons - 1, lons), lax.rem(lon + 1, lons)
    corners = [parts_ref[spot(at), rows:].astype(F32) for at in (after, before)]
    sides = [incoming_ref[spot(at), rows:].astype(F32) for at in (after, before)]
    tall = strip_ref.shape[0]

    def ringed(i):
        inside = 2 <= i < tall - 2
        held, at, step = (sides, i - 2, height) if inside else (corners, i if i < 2 else i - height, 4)
        return jnp.concatenate(
            [strip_ref[i].astype(F32)] + [side[c * step + at : c * step + at + 1] for side in held for c in range(2)]
        )

    windows(
        wide_ref,
        [ringed(0), ringed(1)],
        [lambda r=r: ringed(2 + r) for r in range(height)],
        [ringed(tall - 2), ringed(tall - 1)],
        north,
        south,
    )
    done = activate(conv(wide_ref, 0, height + 6, first_ref), bias_ref, film_ref)
    for r in range(height + 2):
        at = 0 if r == 0 else height + 5 if r == height + 1 else r + 2
        hidden_ref[r] = three(done[at * ring : (at + 1) * ring])
    done = conv(hidden_ref, 0, height, second_ref)
    field_out_ref[...] = main_ref[...]
    lane = lax.broadcasted_iota(jnp.int32, (ring, done.shape[1]), 0)
    tail = width - width // ring * ring
    side = strip_ref.shape[1] // 2
    for r in range(height):
        own = jnp.concatenate([strip_ref[r + 2].astype(F32), jnp.zeros((ring - 2 * side, done.shape[1]), F32)])
        made = own + done[r * ring : (r + 1) * ring]
        field_out_ref[r, :ring] = jnp.where(lane < 2, made, main_ref[r, :ring].astype(F32)).astype(BF16)
        end = made[2 * side - tail : 2 * side]
        field_out_ref[r, width - tail :] = jnp.where(
            lane[:tail] >= tail - 2, end, main_ref[r, width - tail :].astype(F32)
        ).astype(BF16)


def shards(
    fine_field,
    conv_first,
    bias_first,
    film_terms,
    conv_second,
    bottleneck_in,
    query_weight,
    key_weight,
    value_weight,
    out_weight,
):
    lats, lons = lax.axis_size("lat"), lax.axis_size("lon")
    lat, lon = lax.axis_index("lat"), lax.axis_index("lon")
    over_z, over_xc = lat_groups()
    inner, outer = halo_pairs(lats, lons)
    field, tokens = fine_field[0], bottleneck_in[0]
    height, width, channels = field.shape
    rows = tokens.shape[0]

    even = lat % 2 == 0
    step = lats // 4

    turned = [[7, 6, 5, 4, 3, 2, 1, 0]]
    vmem = pl.BlockSpec(memory_space=pltpu.VMEM)
    params = pltpu.CompilerParams(vmem_limit_bytes=VMEM_LIMIT)
    column = lambda c: field[:, c]
    spread = pl.pallas_call(
        spread_body,
        in_specs=[pl.BlockSpec(memory_space=pl.ANY), vmem],
        out_shape=jax.ShapeDtypeStruct((lons, rows + 2 * height, channels), BF16),
        scratch_shapes=[pltpu.VMEM(tokens.shape, BF16), pltpu.SemaphoreType.DMA],
        compiler_params=params,
    )(
        tokens,
        jnp.concatenate([column(c) for c in (0, 1, width - 2, width - 1)]),
    )
    incoming = lax.all_to_all(spread, "lon", 0, 0, axis_index_groups=turned)

    weights = jnp.concatenate([query_weight, key_weight, value_weight], axis=1)
    upper, lower, weights = lax.optimization_barrier((field[:2], field[-2:], weights))
    from_inner = lax.ppermute(jnp.where(even, lower, upper), ("lat", "lon"), inner)
    from_outer = lax.ppermute(jnp.where(even, upper, lower), ("lat", "lon"), outer)

    heads_width = query_weight.shape[1]
    n_z, n_xc = len(over_z[0]), len(over_xc[0])
    queries, pairs = kernel_call(
        project_body,
        (
            jax.ShapeDtypeStruct((rows, heads_width), BF16),
            jax.ShapeDtypeStruct((n_z, rows, 2 * heads_width), BF16),
        ),
    )(incoming, weights)
    pairs = lax.all_to_all(pairs, "lat", 0, 0, axis_index_groups=over_z)
    swap = lambda v, to: lax.ppermute(v, "lat", [(i, to(i // step) * step + i % step) for i in range(lats)])
    near = swap(queries, lambda x: x ^ 1)
    from_inner, from_outer, near = lax.optimization_barrier((from_inner, from_outer, near))
    above = jnp.where(even, from_outer, from_inner)
    below = jnp.where(even, from_inner, from_outer)
    two = jnp.stack([queries, near])
    own = jnp.concatenate([two, swap(two, lambda x: 3 - x)])
    other = lax.ppermute(own, "lat", [(i, i ^ 1) for i in range(lats)])

    side = 6
    ends = lambda rows: jnp.concatenate([rows[:, :side], rows[:, -side:]], axis=1)
    corners = jnp.concatenate([ends(above), ends(below)])
    strip = jnp.concatenate([corners[:2], ends(field), corners[2:]])
    first_columns = jnp.concatenate([corners[:, 0], corners[:, 1]])
    last_columns = jnp.concatenate([corners[:, -2], corners[:, -1]])
    first_columns, last_columns, own = lax.optimization_barrier((first_columns, last_columns, own))

    partial = pl.pallas_call(
        attend_body,
        in_specs=[pl.BlockSpec(memory_space=pltpu.VMEM)] * 3,
        out_shape=jax.ShapeDtypeStruct((n_xc, rows, 2 * heads_width), BF16),
        compiler_params=pltpu.CompilerParams(vmem_limit_bytes=VMEM_LIMIT),
    )(own, other, pairs)

    partial = lax.all_to_all(partial, "lat", 0, 0, axis_index_groups=over_xc)
    projected = pl.pallas_call(
        merge_body,
        in_specs=[vmem] * 4,
        out_shape=jax.ShapeDtypeStruct((lons, rows + first_columns.shape[0], out_weight.shape[1] // lons), BF16),
        compiler_params=params,
    )(partial, out_weight, first_columns, last_columns)
    projected = lax.all_to_all(projected, "lon", 0, 0, axis_index_groups=turned)

    kernels = (
        conv_first.reshape(3, 3 * channels, channels),
        bias_first.reshape(1, channels),
        film_terms,
        conv_second.reshape(3, 3 * channels, channels),
    )
    ring = -(-width // 16) * 16
    main = pl.pallas_call(
        conv_body,
        in_specs=[vmem] * 7,
        out_shape=jax.ShapeDtypeStruct(field.shape, BF16),
        scratch_shapes=[
            pltpu.VMEM((height + 8, ring, 3 * channels), BF16),
            pltpu.VMEM((height + 2, ring, 3 * channels), BF16),
        ],
        compiler_params=params,
    )(field, from_inner, from_outer, *kernels)
    bottleneck_out, fine_out = pl.pallas_call(
        finish_body,
        in_specs=[vmem] * 9,
        out_shape=(jax.ShapeDtypeStruct(tokens.shape, BF16), jax.ShapeDtypeStruct(field.shape, BF16)),
        scratch_shapes=[
            pltpu.VMEM((height + 8, 2 * side + 4, 3 * channels), BF16),
            pltpu.VMEM((height + 2, 2 * side + 4, 3 * channels), BF16),
        ],
        compiler_params=params,
    )(projected, incoming, tokens, main, strip, *kernels)
    return (fine_out[None], bottleneck_out[None])


def solution(mesh):
    placed = (
        P(None, "lat", "lon", None),
        P(),
        P(),
        P(),
        P(),
        P(None, "lat", "lon"),
        P(None, "lon"),
        P(None, "lon"),
        P(None, "lon"),
        P("lon", None),
    )
    return jax.shard_map(
        shards,
        mesh=mesh,
        in_specs=placed,
        out_specs=(P(None, "lat", "lon", None), P(None, "lat", "lon")),
        check_vma=False,
    )
```

```python
import functools

import jax
import jax.numpy as jnp
from jax import lax
from jax.experimental import pallas as pl
from jax.experimental.pallas import tpu as pltpu
from jax.sharding import PartitionSpec as P

HEAD = 64
BF16 = jnp.bfloat16
F32 = jnp.float32
VMEM_LIMIT = 48 * 1024 * 1024


def lat_groups():
    place = lambda x, z, c: x * 16 + z * 2 + c
    over_z = [[place(x, z, c) for z in (4, 3, 5, 2, 6, 1, 7, 0)] for x in range(4) for c in range(2)]
    over_xc = [[place(x, z, c) for x in range(4) for c in range(2)] for z in range(8)]
    return over_z, over_xc


def halo_pairs(lat, lon):
    inner, outer = [], []
    for i in range(lat):
        for j in range(lon):
            me = i * lon + j
            inner.append((me, (i ^ 1) * lon + j))
            if i in (0, lat - 1):
                outer.append((me, i * lon + (j + lon // 2) % lon))
            else:
                outer.append((me, (i + 1 if i % 2 else i - 1) * lon + j))
    return inner, outer


def place_here():
    return lax.axis_index("lat"), lax.axis_index("lon")


def spot(lon):
    return 7 - lon


def kernel_call(body, out_shape, **extra):
    return pl.pallas_call(
        body,
        out_shape=out_shape,
        compiler_params=pltpu.CompilerParams(vmem_limit_bytes=VMEM_LIMIT),
        **extra,
    )


def spread_body(tokens_hbm, given_ref, out_ref, tokens_ref, sem):
    copy = pltpu.make_async_copy(tokens_hbm, tokens_ref, sem)
    copy.start()
    lon = place_here()[1]
    lons, total = out_ref.shape[:2]
    rows = tokens_ref.shape[0]
    first, last = given_ref[: total - rows].astype(F32), given_ref[total - rows :].astype(F32)
    for j in range(lons):
        out_ref[j, rows:] = jnp.where(spot(lax.rem(lon + 1, lons)) == j, last, first).astype(BF16)
    copy.wait()
    for j in range(lons):
        out_ref[j, :rows] = tokens_ref[...]


def project_body(tokens_ref, weight_ref, q_ref, kv_ref):
    rows = q_ref.shape[0]
    wide = jnp.concatenate([tokens_ref[spot(j), :rows] for j in range(tokens_ref.shape[0])], axis=1).astype(F32)
    normed = (wide * lax.rsqrt(jnp.mean(wide * wide, axis=-1, keepdims=True) + 1e-06)).astype(BF16)
    q_width = q_ref.shape[1]
    flat = jnp.dot(normed, weight_ref[...], preferred_element_type=F32).astype(BF16)
    q_ref[...] = flat[:, :q_width]
    kv = flat[:, q_width:]
    for j in range(kv_ref.shape[0]):
        kv_ref[j] = kv


def attend_body(own_ref, other_ref, kv_ref, o_ref):
    rows, width = own_ref.shape[1:]
    q = jnp.concatenate([own_ref[...], other_ref[...]], axis=0)
    n = q.shape[0]
    q = q.reshape(n * rows, width)
    kv = kv_ref[...].reshape(kv_ref.shape[0] * kv_ref.shape[1], 2 * width)
    scale = 1.0 / HEAD**0.5
    outs = []
    lane = lax.broadcasted_iota(jnp.int32, (n * rows, width), 1)
    tail = jnp.zeros((n * rows, width), F32)
    for h in range(width // HEAD):
        qh = q[:, h * HEAD : (h + 1) * HEAD]
        kh = kv[:, h * HEAD : (h + 1) * HEAD]
        vh = kv[:, width + h * HEAD : width + (h + 1) * HEAD]
        scores = lax.dot_general(qh, kh, (((1,), (1,)), ((), ())), preferred_element_type=F32) * scale
        top = jnp.max(scores, axis=-1, keepdims=True)
        expo = jnp.exp(scores - top)
        total = jnp.sum(expo, axis=-1, keepdims=True)
        outs.append(jnp.dot(expo.astype(BF16), vh, preferred_element_type=F32) / total)
        rest = top + jnp.log(total)
        for part in range(3):
            piece = rest.astype(BF16).astype(F32)
            rest = rest - piece
            tail = jnp.where(lane == 3 * h + part, piece, tail)
    result = jnp.concatenate(outs + [tail], axis=1).astype(BF16)
    lat = place_here()[0]
    x, core = lat // 16, lax.rem(lat, 2)
    for t in range(2):
        for s, chip in enumerate((x, x ^ 1, 3 - x, (3 - x) ^ 1)):
            o_ref[2 * chip + (core ^ t)] = result[(4 * t + s) * rows : (4 * t + s + 1) * rows]


def merge_body(o_ref, wo_ref, first_ref, last_ref, out_ref):
    lon = place_here()[1]
    n, rows, width = o_ref.shape[0], o_ref.shape[1], o_ref.shape[2] // 2
    heads = []
    for h in range(width // HEAD):
        logs = []
        for p in range(n):
            pieces = o_ref[p, :, width : 2 * width].astype(F32)
            logs.append(pieces[:, 3 * h : 3 * h + 1] + pieces[:, 3 * h + 1 : 3 * h + 2] + pieces[:, 3 * h + 2 : 3 * h + 3])
        top = functools.reduce(jnp.maximum, logs)
        num = jnp.zeros((rows, HEAD), F32)
        total = jnp.zeros((rows, 1), F32)
        for p in range(n):
            weight = jnp.exp(logs[p] - top)
            total = total + weight
            num = num + weight * o_ref[p, :, h * HEAD : (h + 1) * HEAD].astype(F32)
        heads.append(num / total)
    attended = jnp.concatenate(heads, axis=1).astype(BF16)
    partial = jnp.dot(attended, wo_ref[...], preferred_element_type=F32).astype(BF16)
    lons = out_ref.shape[0]
    first, last = first_ref[...].astype(F32), last_ref[...].astype(F32)
    for j in range(lons):
        at = spot(j)
        out_ref[at, :rows] = partial[:, j * width : (j + 1) * width]
        out_ref[at, rows:] = jnp.where(lax.rem(lon + 1, lons) == j, last, first).astype(BF16)


def three(row):
    return jnp.concatenate([pltpu.roll(row, 1, 0), row, pltpu.roll(row, row.shape[0] - 1, 0)], axis=1).astype(BF16)


def windows(wide_ref, above, rows, below, north, south):
    height = len(rows)
    wide_ref[0] = three(jnp.where(north, rows[0](), above[0]))
    wide_ref[1] = three(jnp.where(north, above[0], above[1]))
    wide_ref[2] = three(jnp.where(north, above[1], rows[0]()))
    wide_ref[3] = three(jnp.where(north, above[0], above[1]))
    for r in range(height):
        wide_ref[4 + r] = three(rows[r]())
    wide_ref[4 + height] = three(jnp.where(south, below[1], below[0]))
    wide_ref[5 + height] = three(jnp.where(south, below[0], rows[-1]()))
    wide_ref[6 + height] = three(jnp.where(south, below[1], below[0]))
    wide_ref[7 + height] = three(jnp.where(south, rows[-1](), below[1]))


def conv(source, start, count, kernel):
    _, ring, deep = source.shape
    total = None
    for dy in range(3):
        part = source[start + dy : start + dy + count].reshape(count * ring, deep)
        product = jnp.dot(part, kernel[dy], preferred_element_type=F32)
        total = product if total is None else total + product
    return total


def activate(first, bias_ref, film_ref):
    u = (first + bias_ref[...]) * (1.0 + film_ref[0:1]) + film_ref[1:2]
    return (u / (1.0 + jnp.exp(-u))).astype(BF16).astype(F32)


def conv_body(
    field_ref, inner_ref, outer_ref, first_ref, bias_ref, film_ref, second_ref, out_ref, wide_ref, hidden_ref
):
    height, width, channels = field_ref.shape
    ring = wide_ref.shape[1]
    lat = place_here()[0]
    north, south, even = lat == 0, lat == lax.axis_size("lat") - 1, lax.rem(lat, 2) == 0
    gap = jnp.zeros((ring - width, channels), F32)

    def ringed(row):
        return jnp.concatenate([row.astype(F32), gap])

    def halo(i, yes_ref, no_ref):
        return ringed(jnp.where(even, yes_ref[i].astype(F32), no_ref[i].astype(F32)))

    above = [halo(i, outer_ref, inner_ref) for i in range(2)]
    below = [halo(i, inner_ref, outer_ref) for i in range(2)]
    rows = [lambda r=r: ringed(field_ref[r]) for r in range(height)]
    windows(wide_ref, above, rows, below, north, south)

    hidden_ref[0] = three(activate(conv(wide_ref, 0, 1, first_ref), bias_ref, film_ref))
    hidden_ref[height + 1] = three(activate(conv(wide_ref, height + 5, 1, first_ref), bias_ref, film_ref))
    block = 4
    for r in range(0, height, block):
        done = activate(conv(wide_ref, 3 + r, block, first_ref), bias_ref, film_ref)
        for i in range(block):
            hidden_ref[1 + r + i] = three(done[i * ring : (i + 1) * ring])
    for r in range(0, height, block):
        done = conv(hidden_ref, r, block, second_ref)
        for i in range(block):
            out_ref[r + i] = (field_ref[r + i].astype(F32) + done[i * ring : i * ring + width]).astype(BF16)


def finish_body(
    parts_ref,
    incoming_ref,
    tokens_ref,
    main_ref,
    strip_ref,
    first_ref,
    bias_ref,
    film_ref,
    second_ref,
    tokens_out_ref,
    field_out_ref,
    wide_ref,
    hidden_ref,
):
    lons = parts_ref.shape[0]
    rows = tokens_ref.shape[0]
    height, width, _ = main_ref.shape
    ring = wide_ref.shape[1]
    lat, lon = place_here()
    north, south = lat == 0, lat == lax.axis_size("lat") - 1
    shared = parts_ref[0, :rows].astype(F32)
    for j in range(1, lons):
        shared = shared + parts_ref[j, :rows].astype(F32)
    tokens_out_ref[...] = (tokens_ref[...].astype(F32) + shared).astype(BF16)

    before, after = lax.rem(lon + lons - 1, lons), lax.rem(lon + 1, lons)
    corners = [parts_ref[spot(at), rows:].astype(F32) for at in (after, before)]
    sides = [incoming_ref[spot(at), rows:].astype(F32) for at in (after, before)]
    tall = strip_ref.shape[0]

    def ringed(i):
        inside = 2 <= i < tall - 2
        held, at, step = (sides, i - 2, height) if inside else (corners, i if i < 2 else i - height, 4)
        return jnp.concatenate(
            [strip_ref[i].astype(F32)] + [side[c * step + at : c * step + at + 1] for side in held for c in range(2)]
        )

    windows(
        wide_ref,
        [ringed(0), ringed(1)],
        [lambda r=r: ringed(2 + r) for r in range(height)],
        [ringed(tall - 2), ringed(tall - 1)],
        north,
        south,
    )
    done = activate(conv(wide_ref, 0, height + 6, first_ref), bias_ref, film_ref)
    for r in range(height + 2):
        at = 0 if r == 0 else height + 5 if r == height + 1 else r + 2
        hidden_ref[r] = three(done[at * ring : (at + 1) * ring])
    done = conv(hidden_ref, 0, height, second_ref)
    field_out_ref[...] = main_ref[...]
    lane = lax.broadcasted_iota(jnp.int32, (ring, done.shape[1]), 0)
    tail = width - width // ring * ring
    side = strip_ref.shape[1] // 2
    for r in range(height):
        own = jnp.concatenate([strip_ref[r + 2].astype(F32), jnp.zeros((ring - 2 * side, done.shape[1]), F32)])
        made = own + done[r * ring : (r + 1) * ring]
        field_out_ref[r, :ring] = jnp.where(lane < 2, made, main_ref[r, :ring].astype(F32)).astype(BF16)
        end = made[2 * side - tail : 2 * side]
        field_out_ref[r, width - tail :] = jnp.where(
            lane[:tail] >= tail - 2, end, main_ref[r, width - tail :].astype(F32)
        ).astype(BF16)


def shards(
    fine_field,
    conv_first,
    bias_first,
    film_terms,
    conv_second,
    bottleneck_in,
    query_weight,
    key_weight,
    value_weight,
    out_weight,
):
    lats, lons = lax.axis_size("lat"), lax.axis_size("lon")
    lat, lon = lax.axis_index("lat"), lax.axis_index("lon")
    over_z, over_xc = lat_groups()
    inner, outer = halo_pairs(lats, lons)
    field, tokens = fine_field[0], bottleneck_in[0]
    height, width, channels = field.shape
    rows = tokens.shape[0]

    even = lat % 2 == 0
    step = lats // 4

    turned = [[7, 6, 5, 4, 3, 2, 1, 0]]
    vmem = pl.BlockSpec(memory_space=pltpu.VMEM)
    params = pltpu.CompilerParams(vmem_limit_bytes=VMEM_LIMIT)
    column = lambda c: field[:, c]
    spread = pl.pallas_call(
        spread_body,
        in_specs=[pl.BlockSpec(memory_space=pltpu.HBM), vmem],
        out_shape=jax.ShapeDtypeStruct((lons, rows + 2 * height, channels), BF16),
        scratch_shapes=[pltpu.VMEM(tokens.shape, BF16), pltpu.SemaphoreType.DMA],
        compiler_params=params,
    )(
        tokens,
        jnp.concatenate([column(c) for c in (0, 1, width - 2, width - 1)]),
    )
    incoming = lax.all_to_all(spread, "lon", 0, 0, axis_index_groups=turned)

    weights = jnp.concatenate([query_weight, key_weight, value_weight], axis=1)
    upper, lower, weights = lax.optimization_barrier((field[:2], field[-2:], weights))
    from_inner = lax.ppermute(jnp.where(even, lower, upper), ("lat", "lon"), inner)
    from_outer = lax.ppermute(jnp.where(even, upper, lower), ("lat", "lon"), outer)

    heads_width = query_weight.shape[1]
    n_z, n_xc = len(over_z[0]), len(over_xc[0])
    queries, pairs = kernel_call(
        project_body,
        (
            jax.ShapeDtypeStruct((rows, heads_width), BF16),
            jax.ShapeDtypeStruct((n_z, rows, 2 * heads_width), BF16),
        ),
    )(incoming, weights)
    pairs = lax.all_to_all(pairs, "lat", 0, 0, axis_index_groups=over_z)
    swap = lambda v, to: lax.ppermute(v, "lat", [(i, to(i // step) * step + i % step) for i in range(lats)])
    near = swap(queries, lambda x: x ^ 1)
    from_inner, from_outer, near = lax.optimization_barrier((from_inner, from_outer, near))
    above = jnp.where(even, from_outer, from_inner)
    below = jnp.where(even, from_inner, from_outer)
    two = jnp.stack([queries, near])
    own = jnp.concatenate([two, swap(two, lambda x: 3 - x)])
    other = lax.ppermute(own, "lat", [(i, i ^ 1) for i in range(lats)])

    side = 6
    ends = lambda rows: jnp.concatenate([rows[:, :side], rows[:, -side:]], axis=1)
    corners = jnp.concatenate([ends(above), ends(below)])
    strip = jnp.concatenate([corners[:2], ends(field), corners[2:]])
    first_columns = jnp.concatenate([corners[:, 0], corners[:, 1]])
    last_columns = jnp.concatenate([corners[:, -2], corners[:, -1]])
    first_columns, last_columns, own = lax.optimization_barrier((first_columns, last_columns, own))

    partial = pl.pallas_call(
        attend_body,
        in_specs=[pl.BlockSpec(memory_space=pltpu.VMEM)] * 3,
        out_shape=jax.ShapeDtypeStruct((n_xc, rows, 2 * heads_width), BF16),
        compiler_params=pltpu.CompilerParams(vmem_limit_bytes=VMEM_LIMIT),
    )(own, other, pairs)

    partial = lax.all_to_all(partial, "lat", 0, 0, axis_index_groups=over_xc)
    projected = pl.pallas_call(
        merge_body,
        in_specs=[vmem] * 4,
        out_shape=jax.ShapeDtypeStruct((lons, rows + first_columns.shape[0], out_weight.shape[1] // lons), BF16),
        compiler_params=params,
    )(partial, out_weight, first_columns, last_columns)
    projected = lax.all_to_all(projected, "lon", 0, 0, axis_index_groups=turned)

    kernels = (
        conv_first.reshape(3, 3 * channels, channels),
        bias_first.reshape(1, channels),
        film_terms,
        conv_second.reshape(3, 3 * channels, channels),
    )
    ring = -(-width // 16) * 16
    main = pl.pallas_call(
        conv_body,
        in_specs=[vmem] * 7,
        out_shape=jax.ShapeDtypeStruct(field.shape, BF16),
        scratch_shapes=[
            pltpu.VMEM((height + 8, ring, 3 * channels), BF16),
            pltpu.VMEM((height + 2, ring, 3 * channels), BF16),
        ],
        compiler_params=params,
    )(field, from_inner, from_outer, *kernels)
    bottleneck_out, fine_out = pl.pallas_call(
        finish_body,
        in_specs=[vmem] * 9,
        out_shape=(jax.ShapeDtypeStruct(tokens.shape, BF16), jax.ShapeDtypeStruct(field.shape, BF16)),
        scratch_shapes=[
            pltpu.VMEM((height + 8, 2 * side + 4, 3 * channels), BF16),
            pltpu.VMEM((height + 2, 2 * side + 4, 3 * channels), BF16),
        ],
        compiler_params=params,
    )(projected, incoming, tokens, main, strip, *kernels)
    return (fine_out[None], bottleneck_out[None])


def solution(mesh):
    placed = (
        P(None, "lat", "lon", None),
        P(),
        P(),
        P(),
        P(),
        P(None, "lat", "lon"),
        P(None, "lon"),
        P(None, "lon"),
        P(None, "lon"),
        P("lon", None),
    )
    return jax.shard_map(
        shards,
        mesh=mesh,
        in_specs=placed,
        out_specs=(P(None, "lat", "lon", None), P(None, "lat", "lon")),
        check_vma=False,
    )
```
